128 devices in a mesh: gx: 8 (over z, core), yz: 16 (over y, x).
Axes of the slice: x: 4, y: 4, z: 4, core: 2. Of those that a mesh axis runs over, the one named last changes fastest.
Arguments:
- mixture_fractions: float32 [53, 64, 128, 256], P(None, 'gx', 'yz'), may hold values from 0 to 0.2
- thermal_kelvins: float32 [64, 128, 256], P('gx', 'yz'), may hold values from 300 to 2400
- normalized_thrust_load: float32 [64, 128, 256], P('gx', 'yz'), may hold values from 0.85 to 1.15
- fluid_motion_vector: float32 [3, 64, 128, 256], P(None, 'gx', 'yz'), as said below
- diffusion_coefficient: float32 [54], replicated, may hold values from 0.01 to 0.1
- burning_tally: int32 [8, 16], P('gx', 'yz'), may hold values from 1 to 4096, 32768 in all within a row
- burning_location_list: int32 [8, 16, 4096], P('gx', 'yz'), may hold values from 0 to 16383, as said below
- opening_matrix: bfloat16 [55, 1600], replicated, may hold values from -0.875 to 0.875
- opening_offset: float32 [1600], replicated, may hold values from -3 to 3
- secondary_matrix: bfloat16 [1600, 800], replicated, may hold values from -0.15625 to 0.15625
- secondary_offset: float32 [800], replicated, may hold values from -3 to 3
- tertiary_matrix: bfloat16 [800, 400], replicated, may hold values from -0.21875 to 0.21875
- tertiary_offset: float32 [400], replicated, may hold values from -3 to 3
- closing_matrix: bfloat16 [400, 53], replicated, may hold values from -0.3125 to 0.3125
- closing_offset: float32 [53], replicated, may hold values from -3 to 3
- increment_magnitude: float32 [53], replicated, may hold values from 0.002 to 0.02
- formation_heat_ratio: float32 [53], replicated, may hold values from -12288 to 12288
Outputs:
- species_next: float32 [53, 64, 128, 256], P(None, 'gx', 'yz')
- temperature_next: float32 [64, 128, 256], P('gx', 'yz')
The draws below stay inside these ranges and needn't reach their ends.
Inputs may be any that keep to these rules, and one draw needn't show every extreme that they name: In each mesh block the 4096 entries of burning_location_list are distinct cell numbers of that block. `burning_tally`: the counts of each row of mesh blocks along yz sum to exactly 2048 times the number of blocks along yz; some block in each such row holds exactly 4096. `fluid_motion_vector`: the velocities' typical magnitude grows toward the upstream end of the jet (gx index 0); single values are random.
All inputs are finite; a program needn't handle non-finite values. Where the reference program divides by a largest or mean magnitude, that divisor is 1e-20 or more.
Results may differ from the reference program's by a relative error of at most 0.0004.
Values may be sent and summed in bfloat16 or wider, within the bound.
A program may use at most 128 MiB of HBM per device.

```python
import math
import jax
import jax.numpy as jnp
import numpy as np
from jax import lax

SPECIES = 53
H1 = 1600
H2 = 800
H3 = 400
FEAT = 55
CX = 8
CY = 8
CZ = 256
CAP = 4096
BATCH = 2048
STREAMWISE_SIZE = 64
TRANSVERSE_SIZE = 128
LATERAL_SIZE = 256
N_GX = 8
N_YZ = 16


def draw_fluid_motion_vector(key, part):
    key = jax.random.fold_in(key, 11)
    base = jax.random.normal(key, (3, STREAMWISE_SIZE, TRANSVERSE_SIZE, LATERAL_SIZE), jnp.float32)
    position = jnp.arange(STREAMWISE_SIZE, dtype=jnp.float32)
    amplitude = 1.0 + 2.0 * (STREAMWISE_SIZE - 1 - position) / (STREAMWISE_SIZE - 1)
    axial = jnp.zeros((3, 1, 1, 1), jnp.float32).at[0].set(1.0)
    return (base + axial) * amplitude[None, :, None, None]


def draw_burning_location_list(key, part):
    key = jax.random.fold_in(key, 23)
    groups = STREAMWISE_SIZE // CX * (TRANSVERSE_SIZE // CY)
    keys = jax.random.split(key, groups)
    picks = jax.vmap(lambda k: jax.random.permutation(k, CX * CY * CZ)[:CAP])(keys)
    return picks.reshape(STREAMWISE_SIZE // CX, TRANSVERSE_SIZE // CY, CAP).astype(jnp.int32)


def shard_levels(own_key, dims, cuts, low, high):
    level = 1.0
    for axis_at, shards_of in cuts:
        draws = jax.random.uniform(jax.random.fold_in(jax.random.fold_in(own_key, 6), axis_at), (shards_of,), jnp.float32, low / len(cuts), high / len(cuts))
        level = level * jnp.repeat(jnp.exp(draws), dims[axis_at] // shards_of).reshape((-1,) + (1,) * (len(dims) - 1 - axis_at))
    return level


def length_profile(count, total, limit, lean):
    loads = [(1 << 20) // math.isqrt(standing ** lean) + 1 for standing in range(2, count + 1)]
    rest, holding = total - limit - (count - 1), [1] * (count - 1)
    while rest > 0:
        movable = [i for i in range(count - 1) if holding[i] < limit]
        mass, budget = sum([loads[i] for i in movable]), rest
        for i in movable:
            addition = min(limit - holding[i], max(1, budget * loads[i] // mass), rest)
            holding[i] = holding[i] + addition
            rest = rest - addition
    return np.array([limit] + holding)


def uneven(stream_key, amount, total, reach, slope):
    if amount == 2:
        one = jax.random.randint(stream_key, (), max(1, total - reach), min(reach, total - 1) + 1)
        return jnp.stack([one, total - one])
    lengths = jnp.asarray(length_profile(amount, total, reach, slope), jnp.int32)
    couples = (amount - 1) // 2
    donor, receiver = lengths[1:1 + 2 * couples:2], lengths[2:2 + 2 * couples:2]
    margin = jnp.minimum(donor - 1, reach - receiver)
    shifted = jax.random.randint(jax.random.fold_in(stream_key, 1), (couples,), 0, 1 << 20) % (margin + 1)
    lengths = lengths.at[1:1 + 2 * couples:2].set(donor - shifted).at[2:2 + 2 * couples:2].set(receiver + shifted)
    return lengths[jax.random.permutation(jax.random.fold_in(stream_key, 2), amount)]


def scatter_about(key, extent, scale, reach, held_as=jnp.bfloat16):
    values = jax.random.normal(key, extent, jnp.float32) * scale
    return jnp.minimum(jnp.maximum(values, -reach), reach).astype(held_as)


def setup_inputs(seed: int = 0) -> dict:
    key_list = jax.random.split(jax.random.key(seed), 18)
    mixture_fractions = jnp.clip(0.2 * jax.random.uniform(key_list[0], (SPECIES, STREAMWISE_SIZE, TRANSVERSE_SIZE, LATERAL_SIZE), jnp.float32) ** shard_levels(key_list[0], (SPECIES, STREAMWISE_SIZE, TRANSVERSE_SIZE, LATERAL_SIZE), ((1, 8), (2, 16)), -0.2, 0.2), 0.0, 0.2)
    thermal_kelvins = jnp.clip(300.0 + 2100.0 * jax.random.uniform(key_list[1], (STREAMWISE_SIZE, TRANSVERSE_SIZE, LATERAL_SIZE), jnp.float32) ** shard_levels(key_list[1], (STREAMWISE_SIZE, TRANSVERSE_SIZE, LATERAL_SIZE), ((0, 8), (1, 16)), -0.2, 0.2), 300.0, 2400.0)
    normalized_thrust_load = jnp.clip(0.85 + 0.29999995 * jax.random.uniform(key_list[2], (STREAMWISE_SIZE, TRANSVERSE_SIZE, LATERAL_SIZE), jnp.float32) ** shard_levels(key_list[2], (STREAMWISE_SIZE, TRANSVERSE_SIZE, LATERAL_SIZE), ((0, 8), (1, 16)), -0.2, 0.2), 0.85, 1.15)
    fluid_motion_vector = draw_fluid_motion_vector(jax.random.fold_in(key_list[17], 71), 0)
    diffusion_coefficient = jnp.clip(jnp.exp(jax.random.uniform(key_list[4], (SPECIES + 1,), jnp.float32, math.log(0.01), math.log(0.1))), 0.01, 0.1)
    burning_tally = jax.vmap(lambda own: uneven(own, N_YZ, N_YZ * BATCH, CAP, 2))(jax.random.split(key_list[5], N_GX)).reshape((N_GX, N_YZ)).astype(jnp.int32)
    burning_location_list = draw_burning_location_list(jax.random.fold_in(key_list[17], 71), 0)
    opening_matrix = scatter_about(key_list[7], (FEAT, H1), FEAT ** -0.5, 0.875)
    opening_offset = scatter_about(key_list[8], (H1,), 0.5, 3.0, jnp.float32)
    secondary_matrix = scatter_about(key_list[9], (H1, H2), H1 ** -0.5, 0.15625)
    secondary_offset = scatter_about(key_list[10], (H2,), 0.5, 3.0, jnp.float32)
    tertiary_matrix = scatter_about(key_list[11], (H2, H3), H2 ** -0.5, 0.21875)
    tertiary_offset = scatter_about(key_list[12], (H3,), 0.5, 3.0, jnp.float32)
    closing_matrix = scatter_about(key_list[13], (H3, SPECIES), H3 ** -0.5, 0.3125)
    closing_offset = scatter_about(key_list[14], (SPECIES,), 0.5, 3.0, jnp.float32)
    increment_magnitude = jnp.clip(jnp.exp(jax.random.uniform(key_list[15], (SPECIES,), jnp.float32, math.log(0.002), math.log(0.02))), 0.002, 0.02)
    formation_heat_ratio = scatter_about(key_list[16], (SPECIES,), 2000.0, 12288.0, jnp.float32)
    return {"mixture_fractions": mixture_fractions, "thermal_kelvins": thermal_kelvins, "normalized_thrust_load": normalized_thrust_load, "fluid_motion_vector": fluid_motion_vector, "diffusion_coefficient": diffusion_coefficient, "burning_tally": burning_tally, "burning_location_list": burning_location_list, "opening_matrix": opening_matrix, "opening_offset": opening_offset, "secondary_matrix": secondary_matrix, "secondary_offset": secondary_offset, "tertiary_matrix": tertiary_matrix, "tertiary_offset": tertiary_offset, "closing_matrix": closing_matrix, "closing_offset": closing_offset, "increment_magnitude": increment_magnitude, "formation_heat_ratio": formation_heat_ratio}


def upwind(speed, left, right):
    return jnp.where(speed > 0, speed * left, speed * right)


def advance(padded, vel, diffusion_coefficient, step):
    centre = padded[:, 1:-1, 1:-1]
    uc = vel[:, 1:-1, 1:-1]
    xplus = padded[:, 2:, 1:-1]
    xminus = padded[:, :-2, 1:-1]
    yplus = padded[:, 1:-1, 2:]
    yminus = padded[:, 1:-1, :-2]
    zplus = jnp.roll(centre, -1, 3)
    zminus = jnp.roll(centre, 1, 3)
    flux_x = upwind(0.5 * (uc[0] + vel[0, 2:, 1:-1]), centre, xplus) - upwind(0.5 * (vel[0, :-2, 1:-1] + uc[0]), xminus, centre)
    flux_y = upwind(0.5 * (uc[1] + vel[1, 1:-1, 2:]), centre, yplus) - upwind(0.5 * (vel[1, 1:-1, :-2] + uc[1]), yminus, centre)
    flux_z = upwind(0.5 * (uc[2] + jnp.roll(uc[2], -1, 2)), centre, zplus) - upwind(0.5 * (jnp.roll(uc[2], 1, 2) + uc[2]), zminus, centre)
    laplace = xplus + xminus + yplus + yminus + zplus + zminus - 6.0 * centre
    return centre + step * (diffusion_coefficient[:, None, None, None] * laplace - (flux_x + flux_y + flux_z))


def time_step(fastest, diffusion_coefficient):
    return 0.9 / (fastest + 6.0 * jnp.max(diffusion_coefficient))


def normalize(rows):
    nspec = rows.shape[-1] - 2
    centre = jnp.concatenate([jnp.full((nspec,), 0.1, jnp.float32), jnp.array([1350.0, 1.0], jnp.float32)])
    spread = jnp.concatenate([jnp.full((nspec,), 0.06, jnp.float32), jnp.array([600.0, 0.1], jnp.float32)])
    return ((rows - centre) / spread).astype(jnp.bfloat16)


def chemistry(inputs, opening_matrix, opening_offset, secondary_matrix, secondary_offset, tertiary_matrix, tertiary_offset, closing_matrix, closing_offset, increment_magnitude, formation_heat_ratio):
    hidden = jax.nn.gelu(jnp.dot(inputs, opening_matrix, preferred_element_type=jnp.float32) + opening_offset).astype(jnp.bfloat16)
    hidden = jax.nn.gelu(jnp.dot(hidden, secondary_matrix, preferred_element_type=jnp.float32) + secondary_offset).astype(jnp.bfloat16)
    hidden = jax.nn.gelu(jnp.dot(hidden, tertiary_matrix, preferred_element_type=jnp.float32) + tertiary_offset).astype(jnp.bfloat16)
    delta = (jnp.dot(hidden, closing_matrix, preferred_element_type=jnp.float32) + closing_offset) * increment_magnitude
    heat = -jnp.dot(delta, formation_heat_ratio, precision=lax.Precision.HIGHEST)
    return jnp.concatenate([delta, heat[:, None]], axis=1)


def reference(mixture_fractions, thermal_kelvins, normalized_thrust_load, fluid_motion_vector, diffusion_coefficient, burning_tally, burning_location_list, opening_matrix, opening_offset, secondary_matrix, secondary_offset, tertiary_matrix, tertiary_offset, closing_matrix, closing_offset, increment_magnitude, formation_heat_ratio):
    quantity_bundle = jnp.concatenate([mixture_fractions, thermal_kelvins[None]], 0)
    network_features = jnp.concatenate([quantity_bundle, fluid_motion_vector], 0)
    padded = jnp.pad(network_features, ((0, 0), (1, 1), (1, 1), (0, 0)))
    fastest = jnp.max(jnp.sum(jnp.abs(fluid_motion_vector), axis=0))
    step = time_step(fastest, diffusion_coefficient)
    moved = advance(padded[:SPECIES + 1], padded[SPECIES + 1:], diffusion_coefficient, step)
    fluid_snapshot = jnp.concatenate([mixture_fractions, thermal_kelvins[None], normalized_thrust_load[None]], 0)
    blocks = fluid_snapshot.reshape(FEAT, N_GX, CX, N_YZ, CY, LATERAL_SIZE).transpose(1, 3, 0, 2, 4, 5).reshape(N_GX, N_YZ, FEAT, CX * CY * LATERAL_SIZE)
    weights = (opening_matrix, opening_offset, secondary_matrix, secondary_offset, tertiary_matrix, tertiary_offset, closing_matrix, closing_offset, increment_magnitude, formation_heat_ratio)
    total = N_YZ * BATCH

    def group(items):
        block_state, index, count = items
        rows = jnp.take_along_axis(block_state, index[:, None, :], axis=2).transpose(0, 2, 1)
        inputs = normalize(rows)
        slots = jnp.arange(CAP, dtype=jnp.int32)
        valid = slots[None, :] < count[:, None]
        offsets = jnp.cumsum(count) - count
        place = jnp.where(valid, offsets[:, None] + slots[None, :], total).astype(jnp.int32)
        packed = jnp.zeros((total, FEAT), jnp.bfloat16).at[place.reshape(-1)].set(inputs.reshape(-1, FEAT), mode="drop")
        result = chemistry(packed, *weights)
        back = result[jnp.minimum(place, total - 1)] * valid[:, :, None].astype(jnp.float32)

        def scatter_one(idx, vals):
            return jnp.zeros((SPECIES + 1, CX * CY * LATERAL_SIZE), jnp.float32).at[:, idx].add(vals.T)

        return jax.vmap(scatter_one)(index, back)

    change = lax.map(group, (blocks, burning_location_list, burning_tally))
    change = change.reshape(N_GX, N_YZ, SPECIES + 1, CX, CY, LATERAL_SIZE).transpose(2, 0, 3, 1, 4, 5).reshape(SPECIES + 1, STREAMWISE_SIZE, TRANSVERSE_SIZE, LATERAL_SIZE)
    result = moved + change
    return result[:SPECIES], result[SPECIES]
```

```python
import functools
import math

import jax
import jax.numpy as jnp
from jax import lax
from jax.experimental import pallas as pl
from jax.experimental.pallas import tpu as pltpu
from jax.sharding import PartitionSpec as P

f32 = jnp.float32
bf = jnp.bfloat16
i32 = jnp.int32
G = 8
U = 4
C = math.sqrt(2 / math.pi)
MESH = pl.DeviceIdType.MESH


def lane_gather(x, idx):
    return jnp.take_along_axis(x, idx, axis=1, mode="promise_in_bounds")


def prep_kernel(tally, listing, mix, temp, press, vel,
                packed, pos, offs, vmax, xs, ys,
                buf, velbuf, perm_ref, offs_smem, sems, osem):
    copies=[]
    for j in range(2):
        copies.append(pltpu.make_async_copy(mix.at[:, :, :, pl.ds(128*j,128)], buf.at[j, pl.ds(0,53)], sems.at[j]))
        copies.append(pltpu.make_async_copy(temp.at[:, :, pl.ds(128*j,128)], buf.at[j, 53], sems.at[2+j]))
        copies.append(pltpu.make_async_copy(press.at[:, :, pl.ds(128*j,128)], buf.at[j, 54], sems.at[4+j]))
    vc=pltpu.make_async_copy(vel, velbuf, sems.at[6])
    for c in copies: c.start()
    vc.start()
    buf[0,55]=jnp.zeros((8,8,128),f32); buf[1,55]=jnp.zeros((8,8,128),f32)
    n=tally[0,0]
    cells=listing[0]
    slot=lax.broadcasted_iota(i32,(1,4096),1)
    hi=jnp.where(slot<n, cells>>7, -1)
    lo=cells&127
    rows=lax.broadcasted_iota(i32,(128,4096),0)
    a=jnp.where(hi==rows,1.0,0.0).astype(bf)
    b=jnp.where(lo==rows,1.0,0.0).astype(bf)
    nt=(((1,),(1,)),((),()))
    mask=lax.dot_general(a,b,nt,preferred_element_type=f32)
    maskb=mask.astype(bf)
    ri=lax.broadcasted_iota(i32,(128,128),0); ci=lax.broadcasted_iota(i32,(128,128),1)
    incl=jnp.dot(maskb,jnp.where(ri<=ci,1.0,0.0).astype(bf),preferred_element_type=f32)
    cnt=jnp.dot(maskb,jnp.ones((128,128),bf),preferred_element_type=f32)
    off=jnp.dot(jnp.where(ci<ri,1.0,0.0).astype(bf),cnt.astype(bf),preferred_element_type=f32)
    cntr=lax.dot_general(jnp.ones((8,128),bf),maskb,nt,preferred_element_type=f32)
    up=jnp.where(lax.broadcasted_iota(i32,(128,256),0)<lax.broadcasted_iota(i32,(128,256),1),1.0,0.0).astype(bf)
    offr=jnp.dot(cntr.astype(bf),up,preferred_element_type=f32)
    offs[...]=offr.astype(i32)
    oc=pltpu.make_async_copy(offs, offs_smem, osem)
    oc.start()
    pos[...]=jnp.where(mask>0.5,(off+incl).astype(i32)-1,-1)
    want=(((ci-off.astype(i32))&127)+1).astype(f32)
    at=jnp.zeros((128,128),i32)
    for s in (64,32,16,8,4,2,1):
        v=lane_gather(incl,at+(s-1))
        at=jnp.where(v<want,at+s,at)
    perm_ref[...]=at
    oc.wait()
    vc.wait()
    s=jnp.abs(velbuf[0])+jnp.abs(velbuf[1])+jnp.abs(velbuf[2])
    s=jnp.max(s,axis=0)
    vmax[...]=jnp.maximum(s[:,:128],s[:,128:])
    for c in copies: c.wait()
    flat=buf.reshape(2*56*64,128)
    lane=lax.broadcasted_iota(i32,(56,128),1)
    def group(i,cur):
        gs=[]
        for k in range(G):
            r=i*G+k
            g=flat[pl.ds((k&1)*3584+i*(G//2)+(k>>1),56,stride=64),:]
            gs.append(lane_gather(g,jnp.broadcast_to(perm_ref[pl.ds(r,1),:],(56,128))))
        for k in range(G):
            r=i*G+k
            o=offs_smem[0,r]
            nx=offs_smem[0,r+1]
            t=o>>7
            cur=jnp.where(lane>=(o&127),gs[k],cur)
            packed[t]=cur
            cur=jnp.where((nx>>7)!=t,gs[k],cur)
        return cur
    cur=lax.fori_loop(0,128//G,group,jnp.zeros((56,128),f32),unroll=U)
    packed[n>>7]=cur
    for k,x in enumerate((0,7)):
        for j in range(2):
            xs[k,:54,:,128*j:128*j+128]=buf[j,:54,x]
            xs[k,54,:,128*j:128*j+128]=velbuf[0,x,:,128*j:128*j+128]
    for k,y in enumerate((0,7)):
        for j in range(2):
            ys[k,:54,:,128*j:128*j+128]=flat[pl.ds(j*3584+y,54*8,stride=8),:].reshape(54,8,128)
            ys[k,54,:,128*j:128*j+128]=velbuf[1,:,y,128*j:128*j+128]

def prep(tally,listing,mix,temp,press,vel):
    V=pl.BlockSpec(memory_space=pltpu.VMEM); A=pl.BlockSpec(memory_space=pl.ANY); S=pl.BlockSpec(memory_space=pltpu.SMEM)
    sd=jax.ShapeDtypeStruct
    return pl.pallas_call(prep_kernel,
        out_shape=(sd((33,56,128),f32),sd((128,128),i32),sd((8,256),i32),sd((8,128),f32),sd((2,55,8,256),f32),sd((2,55,8,256),f32)),
        in_specs=[S,V,A,A,A,A],out_specs=[V]*6,
        scratch_shapes=[pltpu.VMEM((2,56,8,8,128),f32),pltpu.VMEM((3,8,8,256),f32),pltpu.VMEM((128,128),i32),pltpu.SMEM((8,256),i32),pltpu.SemaphoreType.DMA((7,)),pltpu.SemaphoreType.DMA],
        compiler_params=pltpu.CompilerParams(vmem_limit_bytes=48<<20),name="prep")(tally,listing,mix,temp,press,vel)


NT = 8


def act(y, s):
    y2 = y * y
    u = y * ((C * 0.044715 / s**3) * y2 + (C / s))
    return (y + y * jnp.tanh(u)).astype(bf)


def col(row, n):
    return jnp.transpose(jnp.broadcast_to(row, (128, n)))


def wide(b, n):
    return jnp.concatenate([b] * (n // 128), axis=1)


def chem_kernel(packed, vmax, xs, ys, w1, b1, w2t, b2, w3t, b3, w4t, b4, inc, hr,
                out, gm, hx, hy,
                w1t, c2, c3, c4, s1, s2, m1, ssem1, rsem1, ssem2, rsem2, hsend, hrecv, *, nx, ny):
    gx, yz = lax.axis_index("gx"), lax.axis_index("yz")
    xpart = [(lax.rem(gx + k, nx), yz) for k in range(1, nx)]
    ypart = [(gx, lax.rem(yz + k, ny)) for k in range(1, ny)]
    barrier = pltpu.get_barrier_semaphore()
    for dev in xpart + ypart:
        pl.semaphore_signal(barrier, inc=1, device_id=dev, device_id_type=MESH)

    b = b1[...].reshape(1, 1600)
    hi = b.astype(bf).astype(f32)
    mid = (b - hi).astype(bf).astype(f32)
    lo = b - hi - mid
    wp = jnp.concatenate([w1[...].astype(f32), hi, mid, lo, jnp.zeros((70, 1600), f32)], axis=0)
    w1t[...] = jnp.transpose(wp)[:, :64].astype(bf)
    c2[...] = col(2.0 * b2[...].reshape(1, 800), 800)
    c3[...] = col(4.0 * b3[...].reshape(1, 400), 400)
    z = jnp.zeros((1, 3), f32)
    c4[0] = col(jnp.concatenate([8.0 * b4[...].reshape(1, 53), z], 1), 56)
    c4[1] = col(jnp.concatenate([inc[...].reshape(1, 53) * 0.125, z], 1), 56)
    c4[2] = col(jnp.concatenate([-hr[...].reshape(1, 53), z], 1), 56)
    n = NT * 128
    r = lax.broadcasted_iota(i32, (56, 1), 0)
    ce = jnp.where(r < 53, 0.1, jnp.where(r == 53, 1350.0, 1.0)).astype(f32)
    sp = jnp.where(r < 53, 0.06, jnp.where(r == 53, 600.0, 0.1)).astype(f32)
    tail = jnp.where(lax.broadcasted_iota(i32, (8, n), 0) < 2, 1.0, 0.0).astype(f32)
    rr = lax.broadcasted_iota(i32, (56, n), 0)

    def block(i, c):
        x = jnp.concatenate([packed[NT * i + k] for k in range(NT)], axis=1)
        x = jnp.where(r < 55, (x - ce) / sp, 1.0)
        x = jnp.concatenate([x, tail], axis=0).astype(bf)
        h = act(jnp.dot(w1t[...], x, preferred_element_type=f32), 1.0)
        a = jnp.dot(w2t[...], h, preferred_element_type=f32) + wide(c2[...], n)
        h = act(a, 2.0)
        a = jnp.dot(w3t[...], h, preferred_element_type=f32) + wide(c3[...], n)
        h = act(a, 4.0)
        a = jnp.dot(w4t[...], h, preferred_element_type=f32)
        a = jnp.concatenate([a, jnp.zeros((3, n), f32)], axis=0)
        d = (a + wide(c4[0], n)) * wide(c4[1], n)
        heat = jnp.sum(d * wide(c4[2], n), axis=0, keepdims=True)
        d = jnp.where(rr == 53, heat, d)
        for k in range(NT):
            out[NT * i + k] = d[:, k * 128:(k + 1) * 128]
        return c

    up_x, down_x = xpart[0], xpart[nx - 2]
    up_y, down_y = ypart[0], ypart[ny - 2]
    remote = lambda src, dst, a, b, dev: pltpu.make_async_remote_copy(
        src_ref=src, dst_ref=dst, send_sem=a, recv_sem=b, device_id=dev, device_id_type=MESH)
    halos = [remote(ys.at[1], hy.at[0], hsend.at[0], hrecv.at[0], up_y),
             remote(ys.at[0], hy.at[1], hsend.at[1], hrecv.at[1], down_y),
             remote(xs.at[1], hx.at[0], hsend.at[2], hrecv.at[2], up_x),
             remote(xs.at[0], hx.at[1], hsend.at[3], hrecv.at[3], down_x)]
    first = [remote(vmax, s1.at[k], ssem1.at[k], rsem1.at[k], ypart[k]) for k in range(ny - 1)]
    second = [remote(m1, s2.at[k], ssem2.at[k], rsem2.at[k], xpart[k]) for k in range(nx - 1)]

    nb = 32 // NT
    def step(i, c):
        @pl.when(i == 0)
        def _():
            pl.semaphore_wait(barrier, nx + ny - 2)
            for cp in first + halos:
                cp.start()

        @pl.when(i == 1)
        def _():
            for cp in first:
                cp.wait()
            m1[...] = jnp.maximum(vmax[...], jnp.max(s1[...], axis=0))
            for cp in second:
                cp.start()

        @pl.when(i == nb - 1)
        def _():
            for cp in second:
                cp.wait()
            gm[...] = jnp.maximum(m1[...], jnp.max(s2[...], axis=0))

        return block(i, c)

    lax.fori_loop(0, nb, step, 0)
    for cp in halos:
        cp.wait()


def chem(nx, ny, packed, vmax, xs, ys, w1, b1, w2, b2, w3, b3, w4, b4, inc, hr):
    V = pl.BlockSpec(memory_space=pltpu.VMEM)
    A = pl.BlockSpec(memory_space=pl.ANY)
    sd = jax.ShapeDtypeStruct
    sem = pltpu.SemaphoreType.DMA
    return pl.pallas_call(
        functools.partial(chem_kernel, nx=nx, ny=ny),
        out_shape=(sd((33, 56, 128), f32), sd((8, 128), f32), sd((2, 55, 8, 256), f32), sd((2, 55, 8, 256), f32)),
        in_specs=[V, V, A, A] + [V] * 10,
        out_specs=[V, V, A, A],
        scratch_shapes=[
            pltpu.VMEM((1600, 64), bf), pltpu.VMEM((800, 128), f32), pltpu.VMEM((400, 128), f32),
            pltpu.VMEM((3, 56, 128), f32),
            pltpu.VMEM((ny - 1, 8, 128), f32), pltpu.VMEM((nx - 1, 8, 128), f32), pltpu.VMEM((8, 128), f32),
            sem((ny - 1,)), sem((ny - 1,)), sem((nx - 1,)), sem((nx - 1,)), sem((4,)), sem((4,)),
        ],
        compiler_params=pltpu.CompilerParams(vmem_limit_bytes=48 << 20, collective_id=0, has_side_effects=True),
        name="chem",
    )(packed, vmax, xs, ys, w1, b1, w2.T, b2, w3.T, b3, w4.T, b4, inc, hr)


def edges(nx, ny):
    gx, yz = lax.axis_index("gx"), lax.axis_index("yz")
    flag = lambda c: jnp.where(c, 1.0, 0.0).astype(f32)
    return flag(gx > 0), flag(gx < nx - 1), flag(yz > 0), flag(yz < ny - 1)


FB=8
def finish_kernel(offs, kappa, gm, pos, d, hx, hy, vel, temp, mix, out, tout, coef, ebuf, dtv, *, edges):
    step=pl.program_id(0)
    flat=ebuf.reshape(2*56*64,128)
    lo_x,hi_x,lo_y,hi_y=edges()
    @pl.when(step==0)
    def _():
        kmax=lax.fori_loop(1,54,lambda k,c: jnp.maximum(c,kappa[k]),kappa[0])
        m=jnp.max(gm[...])
        dt=0.9/(jnp.full((8,256),m)+6.0*kmax)
        dtv[...]=dt
        rows=lax.broadcasted_iota(i32,(8,256),0)
        for x in range(8):
            u0=vel[0,x]; u1=vel[1,x]; u2=vel[2,x]
            xp=vel[0,x+1] if x<7 else hx[1,54]*hi_x
            xm=vel[0,x-1] if x>0 else hx[0,54]*lo_x
            yp=jnp.where(rows==7,hy[1,54,x:x+1,:]*hi_y,pltpu.roll(u1,7,0))
            ym=jnp.where(rows==0,hy[0,54,x:x+1,:]*lo_y,pltpu.roll(u1,1,0))
            zp=pltpu.roll(u2,255,1); zm=pltpu.roll(u2,1,1)
            h=0.5*dt
            c0=jnp.ones((8,256),f32)
            for k,(u,p,q) in enumerate(((u0,xp,xm),(u1,yp,ym),(u2,zp,zm))):
                wp=h*(u+p); wm=h*(q+u)
                coef[2*k,x]=-jnp.minimum(wp,0.0)
                coef[2*k+1,x]=jnp.maximum(wm,0.0)
                c0=c0-(jnp.maximum(wp,0.0)-jnp.minimum(wm,0.0))
            coef[6,x]=c0
        lane=lax.broadcasted_iota(i32,(56,128),1)
        G=8
        def group(i,c):
            gs=[]
            for k in range(G):
                r=i*G+k
                o=offs[0,r]
                t=o>>7
                m=jnp.where(lane>=(o&127),d[t],d[jnp.minimum(t+1,32)])
                p=jnp.broadcast_to(pos[pl.ds(r,1),:],(56,128))
                g=lane_gather(m,p&127)
                gs.append(jnp.where(p>=0,g,0.0))
            for k in range(G):
                flat[pl.ds((k&1)*3584+i*(G//2)+(k>>1),56,stride=64),:]=gs[k]
            return c
        lax.fori_loop(0,128//G,group,0,unroll=2)
    rows=lax.broadcasted_iota(i32,(8,256),0)
    def field(f, load, store):
        kd=kappa[f]*dtv[...]
        hyl=hy[0,f]*lo_y; hyh=hy[1,f]*hi_y
        c6=6.0*kd
        for x in range(8):
            v=load(x)
            xp=load(x+1) if x<7 else hx[1,f]*hi_x
            xm=load(x-1) if x>0 else hx[0,f]*lo_x
            yp=jnp.where(rows==7,hyh[x:x+1,:],pltpu.roll(v,7,0))
            ym=jnp.where(rows==0,hyl[x:x+1,:],pltpu.roll(v,1,0))
            zp=pltpu.roll(v,255,1); zm=pltpu.roll(v,1,1)
            acc=(coef[6,x]-c6)*v
            for k,n in enumerate((xp,xm,yp,ym,zp,zm)):
                acc=acc+(coef[k,x]+kd)*n
            e=jnp.concatenate([ebuf[0,f,x],ebuf[1,f,x]],axis=1)
            store(x,acc+e)
    def loop(i,c):
        def st(x,v): out[i,x]=v
        field(step*FB+i,lambda x: mix[i,x],st)
        return c
    @pl.when(step<6)
    def _():
        lax.fori_loop(0,FB,loop,0)
    @pl.when(step==6)
    def _():
        lax.fori_loop(0,5,loop,0)
        def st(x,v): tout[x]=v
        field(53,lambda x: temp[x],st)

def finish(edges,offs,kappa,gm,pos,d,hx,hy,vel,temp,mix):
    V=pl.BlockSpec(memory_space=pltpu.VMEM); S=pl.BlockSpec(memory_space=pltpu.SMEM)
    sd=jax.ShapeDtypeStruct
    full=lambda a: pl.BlockSpec(a.shape,lambda i,n=a.ndim:(0,)*n)
    blk=pl.BlockSpec((FB,8,8,256),lambda i:(i,0,0,0))
    return pl.pallas_call(functools.partial(finish_kernel,edges=edges),
        grid=(7,),
        out_shape=(sd((53,8,8,256),f32),sd((8,8,256),f32)),
        in_specs=[S,S]+[V]*7+[blk],out_specs=[blk,pl.BlockSpec((8,8,256),lambda i:(0,0,0))],
        scratch_shapes=[pltpu.VMEM((7,8,8,256),f32),pltpu.VMEM((2,56,8,8,128),f32),pltpu.VMEM((8,256),f32)],
        compiler_params=pltpu.CompilerParams(vmem_limit_bytes=48<<20),name="finish")(offs,kappa,gm,pos,d,hx,hy,vel,temp,mix)


def shards(nx, ny, mix, temp, press, vel, kappa, tally, listing, *weights):
    packed, pos, offs, vmax, xs, ys = prep(tally, listing, mix, temp, press, vel)
    d, gm, hx, hy = chem(nx, ny, packed, vmax, xs, ys, *weights)
    return finish(functools.partial(edges, nx, ny), offs, kappa, gm, pos, d, hx, hy, vel, temp, mix)


def solution(mesh):
    in_specs = (
        P(None, "gx", "yz", None),
        P("gx", "yz", None),
        P("gx", "yz", None),
        P(None, "gx", "yz", None),
        P(),
        P("gx", "yz"),
        P("gx", "yz", None),
    ) + (P(),) * 10
    out_specs = (P(None, "gx", "yz", None), P("gx", "yz", None))
    nx, ny = mesh.shape["gx"], mesh.shape["yz"]
    return jax.shard_map(functools.partial(shards, nx, ny), mesh=mesh, in_specs=in_specs, out_specs=out_specs, check_vma=False)
```

```python
import functools
import math

import jax
import jax.numpy as jnp
from jax import lax
from jax.experimental import pallas as pl
from jax.experimental.pallas import tpu as pltpu
from jax.sharding import PartitionSpec as P

f32 = jnp.float32
bf = jnp.bfloat16
i32 = jnp.int32
C = math.sqrt(2 / math.pi)
MESH = pl.DeviceIdType.MESH
VMEM = pl.BlockSpec(memory_space=pltpu.VMEM)
SMEM = pl.BlockSpec(memory_space=pltpu.SMEM)
HBM = pl.BlockSpec(memory_space=pltpu.HBM)
sd = jax.ShapeDtypeStruct
dma = pltpu.SemaphoreType.DMA
G = 8
NT = 8
PITCH = 72
HALF = 56 * PITCH


def lane_gather(x, idx):
    return jnp.take_along_axis(x, idx, axis=1, mode="promise_in_bounds")


def groups(x):
    return [x[8 * k:8 * k + 8] for k in range(7)]


def start_row(i, k):
    return (k & 1) * HALF + i * (G // 2) + (k >> 1)


def prep_kernel(tally, listing, mix, temp, press, vel,
                packed, pos, offs, vmax, xs, ys,
                buf, velbuf, lst, perm_ref, offs_smem, sems, lsem, osem):
    lc = pltpu.make_async_copy(listing.at[0], lst, lsem)
    lc.start()
    copies = [pltpu.make_async_copy(vel, velbuf, sems.at[6])]
    for j in range(2):
        lanes = pl.ds(128 * j, 128)
        copies.append(pltpu.make_async_copy(mix.at[:, :, :, lanes], buf.at[j, pl.ds(0, 53), pl.ds(0, 8)], sems.at[j]))
        copies.append(pltpu.make_async_copy(temp.at[:, :, lanes], buf.at[j, 53, pl.ds(0, 8)], sems.at[2 + j]))
        copies.append(pltpu.make_async_copy(press.at[:, :, lanes], buf.at[j, 54, pl.ds(0, 8)], sems.at[4 + j]))
    for c in copies:
        c.start()
    buf[0, 55] = jnp.zeros((9, 8, 128), f32)
    buf[1, 55] = jnp.zeros((9, 8, 128), f32)
    n = tally[0, 0]
    lc.wait()
    cells = lst[...]
    slot = lax.broadcasted_iota(i32, (1, 4096), 1)
    hi = jnp.where(slot < n, cells >> 7, -1)
    lo = cells & 127
    rows = lax.broadcasted_iota(i32, (128, 4096), 0)
    a = jnp.where(hi == rows, 1.0, 0.0).astype(bf)
    b = jnp.where(lo == rows, 1.0, 0.0).astype(bf)
    nt = (((1,), (1,)), ((), ()))
    mask = lax.dot_general(a, b, nt, preferred_element_type=f32)
    maskb = mask.astype(bf)
    ri = lax.broadcasted_iota(i32, (128, 128), 0)
    ci = lax.broadcasted_iota(i32, (128, 128), 1)
    before = lax.broadcasted_iota(i32, (128, 256), 0) < lax.broadcasted_iota(i32, (128, 256), 1)
    cntr = lax.dot_general(jnp.ones((8, 128), bf), maskb, nt, preferred_element_type=f32)
    offs[...] = jnp.dot(cntr.astype(bf), jnp.where(before, 1.0, 0.0).astype(bf), preferred_element_type=f32).astype(i32)
    oc = pltpu.make_async_copy(offs, offs_smem, osem)
    oc.start()
    incl = jnp.dot(maskb, jnp.where(ri <= ci, 1.0, 0.0).astype(bf), preferred_element_type=f32)
    cnt = jnp.dot(maskb, jnp.ones((128, 128), bf), preferred_element_type=f32)
    off = jnp.dot(jnp.where(ci < ri, 1.0, 0.0).astype(bf), cnt.astype(bf), preferred_element_type=f32)
    pos[...] = jnp.where(mask > 0.5, (off + incl).astype(i32) - 1, -1)
    want = (((ci - off.astype(i32)) & 127) + 1).astype(f32)
    at = jnp.zeros((128, 128), i32)
    for s in (64, 32, 16, 8, 4, 2, 1):
        v = lane_gather(incl, at + (s - 1))
        at = jnp.where(v < want, at + s, at)
    perm_ref[...] = at
    copies[0].wait()
    s = jnp.abs(velbuf[0]) + jnp.abs(velbuf[1]) + jnp.abs(velbuf[2])
    s = jnp.max(s, axis=0)
    vmax[...] = jnp.maximum(s[:, :128], s[:, 128:])
    for c in copies[1:]:
        c.wait()
    oc.wait()
    flat = buf.reshape(2 * HALF, 128)
    lane = lax.broadcasted_iota(i32, (8, 128), 1)

    def group(i, cur):
        gs = []
        for k in range(G):
            g = flat[pl.ds(start_row(i, k), 56, stride=PITCH), :]
            p = jnp.broadcast_to(perm_ref[pl.ds(i * G + k, 1), :], (8, 128))
            gs.append([lane_gather(x, p) for x in groups(g)])
        for k in range(G):
            o = offs_smem[0, i * G + k]
            t = o >> 7
            m = lane >= (o & 127)
            fresh = (offs_smem[0, i * G + k + 1] >> 7) != t
            cur = [jnp.where(m, g, c) for g, c in zip(gs[k], cur)]
            for q in range(7):
                packed[t, 8 * q:8 * q + 8] = cur[q]
            cur = [jnp.where(fresh, g, c) for g, c in zip(gs[k], cur)]
        return tuple(cur)

    cur = lax.fori_loop(0, 128 // G, group, tuple(jnp.zeros((8, 128), f32) for _ in range(7)), unroll=4)
    for q in range(7):
        packed[n >> 7, 8 * q:8 * q + 8] = cur[q]
    for k, x in enumerate((0, 7)):
        u = velbuf[0, x]
        uh = u.astype(bf).astype(f32)
        xs[k, 432:448] = jnp.concatenate([uh, u - uh], axis=0).astype(bf)
        for j in range(2):
            xs[k, 0:432, 128 * j:128 * j + 128] = buf[j, 0:54, x].reshape(432, 128).astype(bf)
    for k, y in enumerate((0, 7)):
        u = velbuf[1, :, y, :]
        uh = u.astype(bf).astype(f32)
        ys[k, 432:448] = jnp.concatenate([uh, u - uh], axis=0).astype(bf)
        for j in range(2):
            for f in range(0, 54, 2):
                z = [flat[pl.ds(j * HALF + (f + q) * PITCH + y, 8, stride=8), :] for q in range(2)]
                ys[k, 8 * f:8 * f + 16, 128 * j:128 * j + 128] = jnp.concatenate(z, axis=0).astype(bf)


def in_hbm(*arrays):
    return [pltpu.with_memory_space_constraint(a, pltpu.HBM) for a in arrays]


def prep(tally, listing, mix, temp, press, vel):
    return pl.pallas_call(
        prep_kernel,
        out_shape=(sd((33, 56, 128), f32), sd((128, 128), i32), sd((8, 256), i32), sd((8, 128), f32),
                   sd((2, 448, 256), bf), sd((2, 448, 256), bf)),
        in_specs=[SMEM] + [HBM] * 5,
        out_specs=[VMEM] * 6,
        scratch_shapes=[pltpu.VMEM((2, 56, 9, 8, 128), f32), pltpu.VMEM((3, 8, 8, 256), f32), pltpu.VMEM((1, 4096), i32),
                        pltpu.VMEM((128, 128), i32), pltpu.SMEM((8, 256), i32), dma((7,)), dma, dma],
        compiler_params=pltpu.CompilerParams(vmem_limit_bytes=20 << 20),
        name="prep",
    )(tally, *in_hbm(listing, mix, temp, press, vel))


def act(y, s):
    y2 = y * y
    u = y * ((C * 0.044715 / s**3) * y2 + (C / s))
    return (y + y * jnp.tanh(u)).astype(bf)


def col(row, n):
    return jnp.transpose(jnp.broadcast_to(row, (128, n)))


def wide(b, n):
    return jnp.concatenate([b] * (n // 128), axis=1)


def chem_kernel(packed, vmax, xs, ys, w1, b1, w2t, b2, w3t, b3, w4t, b4, inc, hr,
                out, gm, hx, hy,
                w1t, c2, c3, c4, s1, s2, m1, ssem1, rsem1, ssem2, rsem2, hsend, hrecv, *, nx, ny):
    gx, yz = lax.axis_index("gx"), lax.axis_index("yz")
    xpart = [(lax.rem(gx + k, nx), yz) for k in range(1, nx)]
    ypart = [(gx, lax.rem(yz + k, ny)) for k in range(1, ny)]
    barrier = pltpu.get_barrier_semaphore()
    for dev in xpart + ypart:
        pl.semaphore_signal(barrier, inc=1, device_id=dev, device_id_type=MESH)

    b = b1[...].reshape(1, 1600)
    hi = b.astype(bf).astype(f32)
    mid = (b - hi).astype(bf).astype(f32)
    lo = b - hi - mid
    wp = jnp.concatenate([w1[...].astype(f32), hi, mid, lo, jnp.zeros((70, 1600), f32)], axis=0)
    w1t[...] = jnp.transpose(wp)[:, :64].astype(bf)
    c2[...] = col(2.0 * b2[...].reshape(1, 800), 800)
    c3[...] = col(4.0 * b3[...].reshape(1, 400), 400)
    z = jnp.zeros((1, 3), f32)
    c4[0] = col(jnp.concatenate([8.0 * b4[...].reshape(1, 53), z], 1), 56)
    c4[1] = col(jnp.concatenate([inc[...].reshape(1, 53) * 0.125, z], 1), 56)
    c4[2] = col(jnp.concatenate([-hr[...].reshape(1, 53), z], 1), 56)
    n = NT * 128
    r = lax.broadcasted_iota(i32, (56, 1), 0)
    ce = jnp.where(r < 53, 0.1, jnp.where(r == 53, 1350.0, 1.0)).astype(f32)
    sp = jnp.where(r < 53, 0.06, jnp.where(r == 53, 600.0, 0.1)).astype(f32)
    tail = jnp.where(lax.broadcasted_iota(i32, (8, n), 0) < 2, 1.0, 0.0).astype(f32)
    rr = lax.broadcasted_iota(i32, (56, n), 0)

    up_x, down_x = xpart[0], xpart[nx - 2]
    up_y, down_y = ypart[0], ypart[ny - 2]
    remote = lambda src, dst, a, b, dev: pltpu.make_async_remote_copy(
        src_ref=src, dst_ref=dst, send_sem=a, recv_sem=b, device_id=dev, device_id_type=MESH)
    halos = [remote(ys.at[1], hy.at[0], hsend.at[0], hrecv.at[0], up_y),
             remote(ys.at[0], hy.at[1], hsend.at[1], hrecv.at[1], down_y),
             remote(xs.at[1], hx.at[0], hsend.at[2], hrecv.at[2], up_x),
             remote(xs.at[0], hx.at[1], hsend.at[3], hrecv.at[3], down_x)]
    first = [remote(vmax, s1.at[k], ssem1.at[k], rsem1.at[k], ypart[k]) for k in range(ny - 1)]
    second = [remote(m1, s2.at[k], ssem2.at[k], rsem2.at[k], xpart[k]) for k in range(nx - 1)]

    def exchange(i):
        @pl.when(i == 1)
        def _():
            pl.semaphore_wait(barrier, nx + ny - 2)
            for cp in first + halos:
                cp.start()

        @pl.when(i == 2)
        def _():
            for cp in first:
                cp.wait()
            m1[...] = jnp.maximum(vmax[...], jnp.max(s1[...], axis=0))
            for cp in second:
                cp.start()

    def block(i, c):
        x = jnp.concatenate([packed[NT * i + k] for k in range(NT)], axis=1)
        x = jnp.where(r < 55, (x - ce) / sp, 1.0)
        x = jnp.concatenate([x, tail], axis=0).astype(bf)
        h = act(jnp.dot(w1t[...], x, preferred_element_type=f32), 1.0)
        a = jnp.dot(w2t[...], h, preferred_element_type=f32) + wide(c2[...], n)
        h = act(a, 2.0)
        a = jnp.dot(w3t[...], h, preferred_element_type=f32) + wide(c3[...], n)
        h = act(a, 4.0)
        a = jnp.dot(w4t[...], h, preferred_element_type=f32)
        a = jnp.concatenate([a, jnp.zeros((3, n), f32)], axis=0)
        d = (a + wide(c4[0], n)) * wide(c4[1], n)
        heat = jnp.sum(d * wide(c4[2], n), axis=0, keepdims=True)
        d = jnp.where(rr == 53, heat, d)
        for k in range(NT):
            out[NT * i + k] = d[:, k * 128:(k + 1) * 128]
        exchange(i)
        return c

    lax.fori_loop(0, 32 // NT, block, 0)
    for cp in second:
        cp.wait()
    gm[...] = jnp.maximum(m1[...], jnp.max(s2[...], axis=0))
    for cp in halos:
        cp.wait()


def chem(nx, ny, packed, vmax, xs, ys, w1, b1, w2, b2, w3, b3, w4, b4, inc, hr):
    return pl.pallas_call(
        functools.partial(chem_kernel, nx=nx, ny=ny),
        out_shape=(sd((33, 56, 128), f32), sd((8, 128), f32), sd((2, 448, 256), bf), sd((2, 448, 256), bf)),
        in_specs=[VMEM] * 14,
        out_specs=[VMEM] * 4,
        scratch_shapes=[
            pltpu.VMEM((1600, 64), bf), pltpu.VMEM((800, 128), f32), pltpu.VMEM((400, 128), f32),
            pltpu.VMEM((3, 56, 128), f32),
            pltpu.VMEM((ny - 1, 8, 128), f32), pltpu.VMEM((nx - 1, 8, 128), f32), pltpu.VMEM((8, 128), f32),
            dma((ny - 1,)), dma((ny - 1,)), dma((nx - 1,)), dma((nx - 1,)), dma((4,)), dma((4,)),
        ],
        compiler_params=pltpu.CompilerParams(vmem_limit_bytes=32 << 20, collective_id=0, has_side_effects=True),
        name="chem",
    )(packed, vmax, xs, ys, w1, b1, w2.T, b2, w3.T, b3, w4.T, b4, inc, hr)


def finish_kernel(offs, kappa, kapv, gm, pos, d, hx, hy, vel, temp, mix, out, tout,
                  coef, ebuf, obuf, hxf, hyf, sems, *, edges):
    flat = ebuf.reshape(2 * HALF, 128)
    lo_x, hi_x, lo_y, hi_y = edges()
    rows = lax.broadcasted_iota(i32, (8, 256), 0)
    lane = lax.broadcasted_iota(i32, (8, 128), 1)
    for k, (fx, fy) in enumerate(((lo_x, lo_y), (hi_x, hi_y))):
        hxf[k] = (hx[k].astype(f32) * fx).reshape(56, 8, 256)
        hyf[k] = (hy[k].astype(f32) * fy).reshape(56, 8, 256)
    dt = 0.9 / (jnp.full((8, 256), jnp.max(gm[...])) + 6.0 * jnp.max(kapv[...].reshape(1, 54)))
    h = 0.5 * dt
    ux = [hxf[k, 54] + hxf[k, 55] for k in range(2)]
    uy = [hyf[k, 54] + hyf[k, 55] for k in range(2)]
    for x in range(8):
        u0 = vel[0, x]
        u1 = vel[1, x]
        u2 = vel[2, x]
        xp = vel[0, x + 1] if x < 7 else ux[1]
        xm = vel[0, x - 1] if x > 0 else ux[0]
        yp = jnp.where(rows == 7, uy[1][x:x + 1, :], pltpu.roll(u1, 7, 0))
        ym = jnp.where(rows == 0, uy[0][x:x + 1, :], pltpu.roll(u1, 1, 0))
        zp = pltpu.roll(u2, 255, 1)
        zm = pltpu.roll(u2, 1, 1)
        c0 = jnp.ones((8, 256), f32)
        for k, (u, p, q) in enumerate(((u0, xp, xm), (u1, yp, ym), (u2, zp, zm))):
            wp = h * (u + p)
            wm = h * (q + u)
            coef[2 * k, x] = -jnp.minimum(wp, 0.0)
            coef[2 * k + 1, x] = jnp.maximum(wm, 0.0)
            c0 = c0 - (jnp.maximum(wp, 0.0) - jnp.minimum(wm, 0.0))
        coef[6, x] = c0

    def group(i, c):
        gs = []
        for k in range(G):
            o = offs[0, i * G + k]
            t = o >> 7
            m = lane >= (o & 127)
            p = jnp.broadcast_to(pos[pl.ds(i * G + k, 1), :], (8, 128))
            q = p & 127
            there = p >= 0
            a = groups(d[t])
            b = groups(d[jnp.minimum(t + 1, 32)])
            gs.append([jnp.where(there, lane_gather(jnp.where(m, x, y), q), 0.0) for x, y in zip(a, b)])
        for k in range(G):
            flat[pl.ds(start_row(i, k), 56, stride=PITCH), :] = jnp.concatenate(gs[k], axis=0)
        return c

    lax.fori_loop(0, 128 // G, group, 0, unroll=2)

    def field(f, load, store):
        kd = kappa[f] * dt
        c6 = 6.0 * kd
        hyl = hyf[0, f]
        hyh = hyf[1, f]
        for x in range(8):
            v = load(x)
            xp = load(x + 1) if x < 7 else hxf[1, f]
            xm = load(x - 1) if x > 0 else hxf[0, f]
            yp = jnp.where(rows == 7, hyh[x:x + 1, :], pltpu.roll(v, 7, 0))
            ym = jnp.where(rows == 0, hyl[x:x + 1, :], pltpu.roll(v, 1, 0))
            zp = pltpu.roll(v, 255, 1)
            zm = pltpu.roll(v, 1, 1)
            acc = (coef[6, x] - c6) * v
            for k, nb in enumerate((xp, xm, yp, ym, zp, zm)):
                acc = acc + (coef[k, x] + kd) * nb
            store(x, acc + jnp.concatenate([ebuf[0, f, x], ebuf[1, f, x]], axis=1))

    def one(f, c):
        def st(x, v):
            obuf[f, x] = v
        field(f, lambda x: mix[f, x], st)
        pltpu.make_async_copy(obuf.at[f], out.at[f], sems.at[f]).start()
        return c

    def stt(x, v):
        obuf[53, x] = v
    field(53, lambda x: temp[x], stt)
    pltpu.make_async_copy(obuf.at[53], tout, sems.at[53]).start()
    lax.fori_loop(0, 53, one, 0)

    def drain(f, c):
        pltpu.make_async_copy(obuf.at[f], out.at[f], sems.at[f]).wait()
        return c
    lax.fori_loop(0, 53, drain, 0)
    pltpu.make_async_copy(obuf.at[53], tout, sems.at[53]).wait()


def finish(edges, offs, kappa, gm, pos, d, hx, hy, vel, temp, mix):
    return pl.pallas_call(
        functools.partial(finish_kernel, edges=edges),
        out_shape=(sd((53, 8, 8, 256), f32), sd((8, 8, 256), f32)),
        in_specs=[SMEM, SMEM] + [VMEM] * 9,
        out_specs=[HBM, HBM],
        scratch_shapes=[pltpu.VMEM((7, 8, 8, 256), f32), pltpu.VMEM((2, 56, 9, 8, 128), f32),
                        pltpu.VMEM((54, 8, 8, 256), f32), pltpu.VMEM((2, 56, 8, 256), f32),
                        pltpu.VMEM((2, 56, 8, 256), f32), dma((54,))],
        compiler_params=pltpu.CompilerParams(vmem_limit_bytes=24 << 20),
        name="finish",
    )(offs, kappa, kappa, gm, pos, d, hx, hy, vel, temp, mix)


def edges(nx, ny):
    gx, yz = lax.axis_index("gx"), lax.axis_index("yz")
    flag = lambda c: jnp.where(c, 1.0, 0.0).astype(f32)
    return flag(gx > 0), flag(gx < nx - 1), flag(yz > 0), flag(yz < ny - 1)


def shards(nx, ny, mix, temp, press, vel, kappa, tally, listing, *weights):
    packed, pos, offs, vmax, xs, ys = prep(tally, listing, mix, temp, press, vel)
    d, gm, hx, hy = chem(nx, ny, packed, vmax, xs, ys, *weights)
    return finish(functools.partial(edges, nx, ny), offs, kappa, gm, pos, d, hx, hy, vel, temp, mix)


def solution(mesh):
    in_specs = (
        P(None, "gx", "yz", None),
        P("gx", "yz", None),
        P("gx", "yz", None),
        P(None, "gx", "yz", None),
        P(),
        P("gx", "yz"),
        P("gx", "yz", None),
    ) + (P(),) * 10
    out_specs = (P(None, "gx", "yz", None), P("gx", "yz", None))
    nx, ny = mesh.shape["gx"], mesh.shape["yz"]
    return jax.shard_map(functools.partial(shards, nx, ny), mesh=mesh, in_specs=in_specs, out_specs=out_specs, check_vma=False)
```

```python
import functools
import math

import jax
import jax.numpy as jnp
from jax import lax
from jax.experimental import pallas as pl
from jax.experimental.pallas import tpu as pltpu
from jax.sharding import PartitionSpec as P

f32 = jnp.float32
bf = jnp.bfloat16
i32 = jnp.int32
C = math.sqrt(2 / math.pi)
MESH = pl.DeviceIdType.MESH
VMEM = pl.BlockSpec(memory_space=pltpu.VMEM)
SMEM = pl.BlockSpec(memory_space=pltpu.SMEM)
HBM = pl.BlockSpec(memory_space=pltpu.HBM)
sd = jax.ShapeDtypeStruct
dma = pltpu.SemaphoreType.DMA
G = 8
NT = 8
UF = 4
PITCH = 72
HALF = 56 * PITCH


def lane_gather(x, idx):
    return jnp.take_along_axis(x, idx, axis=1, mode="promise_in_bounds")


def groups(x):
    return [x[8 * k:8 * k + 8] for k in range(7)]


def start_row(i, k):
    return (k & 1) * HALF + i * (G // 2) + (k >> 1)


def prep_kernel(tally, listing, mix, temp, press, vel,
                packed, pos, offs, vmax, xs, ys,
                buf, velbuf, lst, perm_ref, offs_smem, sems, lsem, osem):
    lc = pltpu.make_async_copy(listing.at[0], lst, lsem)
    lc.start()
    copies = [pltpu.make_async_copy(vel, velbuf, sems.at[6])]
    for j in range(2):
        lanes = pl.ds(128 * j, 128)
        copies.append(pltpu.make_async_copy(mix.at[:, :, :, lanes], buf.at[j, pl.ds(0, 53), pl.ds(0, 8)], sems.at[j]))
        copies.append(pltpu.make_async_copy(temp.at[:, :, lanes], buf.at[j, 53, pl.ds(0, 8)], sems.at[2 + j]))
        copies.append(pltpu.make_async_copy(press.at[:, :, lanes], buf.at[j, 54, pl.ds(0, 8)], sems.at[4 + j]))
    for c in copies:
        c.start()
    buf[0, 55] = jnp.zeros((9, 8, 128), f32)
    buf[1, 55] = jnp.zeros((9, 8, 128), f32)
    n = tally[0, 0]
    lc.wait()
    cells = lst[...]
    slot = lax.broadcasted_iota(i32, (1, 4096), 1)
    hi = jnp.where(slot < n, cells >> 7, -1)
    lo = cells & 127
    rows = lax.broadcasted_iota(i32, (128, 4096), 0)
    a = jnp.where(hi == rows, 1.0, 0.0).astype(bf)
    b = jnp.where(lo == rows, 1.0, 0.0).astype(bf)
    nt = (((1,), (1,)), ((), ()))
    mask = lax.dot_general(a, b, nt, preferred_element_type=f32)
    maskb = mask.astype(bf)
    ri = lax.broadcasted_iota(i32, (128, 128), 0)
    ci = lax.broadcasted_iota(i32, (128, 128), 1)
    before = lax.broadcasted_iota(i32, (128, 256), 0) < lax.broadcasted_iota(i32, (128, 256), 1)
    cntr = lax.dot_general(jnp.ones((8, 128), bf), maskb, nt, preferred_element_type=f32)
    offs[...] = jnp.dot(cntr.astype(bf), jnp.where(before, 1.0, 0.0).astype(bf), preferred_element_type=f32).astype(i32)
    oc = pltpu.make_async_copy(offs, offs_smem, osem)
    oc.start()
    incl = jnp.dot(maskb, jnp.where(ri <= ci, 1.0, 0.0).astype(bf), preferred_element_type=f32)
    cnt = jnp.dot(maskb, jnp.ones((128, 128), bf), preferred_element_type=f32)
    off = jnp.dot(jnp.where(ci < ri, 1.0, 0.0).astype(bf), cnt.astype(bf), preferred_element_type=f32)
    pos[...] = jnp.where(mask > 0.5, (off + incl).astype(i32) - 1, -1)
    want = (((ci - off.astype(i32)) & 127) + 1).astype(f32)
    at = jnp.zeros((128, 128), i32)
    for s in (64, 32, 16, 8, 4, 2, 1):
        v = lane_gather(incl, at + (s - 1))
        at = jnp.where(v < want, at + s, at)
    perm_ref[...] = at
    copies[0].wait()
    s = jnp.abs(velbuf[0]) + jnp.abs(velbuf[1]) + jnp.abs(velbuf[2])
    s = jnp.max(s, axis=0)
    vmax[...] = jnp.maximum(s[:, :128], s[:, 128:])
    for c in copies[1:]:
        c.wait()
    oc.wait()
    flat = buf.reshape(2 * HALF, 128)
    lane = lax.broadcasted_iota(i32, (8, 128), 1)

    def group(i, cur):
        gs = []
        for k in range(G):
            g = flat[pl.ds(start_row(i, k), 56, stride=PITCH), :]
            p = jnp.broadcast_to(perm_ref[pl.ds(i * G + k, 1), :], (8, 128))
            gs.append([lane_gather(x, p) for x in groups(g)])
        for k in range(G):
            o = offs_smem[0, i * G + k]
            t = o >> 7
            m = lane >= (o & 127)
            fresh = (offs_smem[0, i * G + k + 1] >> 7) != t
            cur = [jnp.where(m, g, c) for g, c in zip(gs[k], cur)]
            for q in range(7):
                packed[t, 8 * q:8 * q + 8] = cur[q]
            cur = [jnp.where(fresh, g, c) for g, c in zip(gs[k], cur)]
        return tuple(cur)

    cur = lax.fori_loop(0, 128 // G, group, tuple(jnp.zeros((8, 128), f32) for _ in range(7)), unroll=4)
    for q in range(7):
        packed[n >> 7, 8 * q:8 * q + 8] = cur[q]
    for k, x in enumerate((0, 7)):
        u = velbuf[0, x]
        uh = u.astype(bf).astype(f32)
        xs[k, 432:448] = jnp.concatenate([uh, u - uh], axis=0).astype(bf)
        for j in range(2):
            xs[k, 0:432, 128 * j:128 * j + 128] = buf[j, 0:54, x].reshape(432, 128).astype(bf)
    for k, y in enumerate((0, 7)):
        u = velbuf[1, :, y, :]
        uh = u.astype(bf).astype(f32)
        ys[k, 432:448] = jnp.concatenate([uh, u - uh], axis=0).astype(bf)
        for j in range(2):
            for f in range(0, 54, 2):
                z = [flat[pl.ds(j * HALF + (f + q) * PITCH + y, 8, stride=8), :] for q in range(2)]
                ys[k, 8 * f:8 * f + 16, 128 * j:128 * j + 128] = jnp.concatenate(z, axis=0).astype(bf)


def in_hbm(*arrays):
    return [pltpu.with_memory_space_constraint(a, pltpu.HBM) for a in arrays]


def prep(tally, listing, mix, temp, press, vel):
    return pl.pallas_call(
        prep_kernel,
        out_shape=(sd((33, 56, 128), f32), sd((128, 128), i32), sd((8, 256), i32), sd((8, 128), f32),
                   sd((2, 448, 256), bf), sd((2, 448, 256), bf)),
        in_specs=[SMEM] + [HBM] * 5,
        out_specs=[VMEM] * 6,
        scratch_shapes=[pltpu.VMEM((2, 56, 9, 8, 128), f32), pltpu.VMEM((3, 8, 8, 256), f32), pltpu.VMEM((1, 4096), i32),
                        pltpu.VMEM((128, 128), i32), pltpu.SMEM((8, 256), i32), dma((7,)), dma, dma],
        compiler_params=pltpu.CompilerParams(vmem_limit_bytes=20 << 20),
        name="prep",
    )(tally, *in_hbm(listing, mix, temp, press, vel))


def act(y, s):
    y2 = y * y
    u = y * ((C * 0.044715 / s**3) * y2 + (C / s))
    return (y + y * jnp.tanh(u)).astype(bf)


def col(row, n):
    return jnp.transpose(jnp.broadcast_to(row, (128, n)))


def wide(b, n):
    return jnp.concatenate([b] * (n // 128), axis=1)


def chem_kernel(packed, vmax, xs, ys, w1, b1, w2t, b2, w3t, b3, w4t, b4, inc, hr,
                out, gm, hx, hy,
                w1t, c2, c3, c4, s1, s2, m1, ssem1, rsem1, ssem2, rsem2, hsend, hrecv, *, nx, ny):
    gx, yz = lax.axis_index("gx"), lax.axis_index("yz")
    xpart = [(lax.rem(gx + k, nx), yz) for k in range(1, nx)]
    ypart = [(gx, lax.rem(yz + k, ny)) for k in range(1, ny)]
    barrier = pltpu.get_barrier_semaphore()
    for dev in xpart + ypart:
        pl.semaphore_signal(barrier, inc=1, device_id=dev, device_id_type=MESH)

    b = b1[...].reshape(1, 1600)
    hi = b.astype(bf).astype(f32)
    mid = (b - hi).astype(bf).astype(f32)
    lo = b - hi - mid
    wp = jnp.concatenate([w1[...].astype(f32), hi, mid, lo, jnp.zeros((70, 1600), f32)], axis=0)
    w1t[...] = jnp.transpose(wp)[:, :64].astype(bf)
    c2[...] = col(2.0 * b2[...].reshape(1, 800), 800)
    c3[...] = col(4.0 * b3[...].reshape(1, 400), 400)
    z = jnp.zeros((1, 3), f32)
    c4[0] = col(jnp.concatenate([8.0 * b4[...].reshape(1, 53), z], 1), 56)
    c4[1] = col(jnp.concatenate([inc[...].reshape(1, 53) * 0.125, z], 1), 56)
    c4[2] = col(jnp.concatenate([-hr[...].reshape(1, 53), z], 1), 56)
    n = NT * 128
    r = lax.broadcasted_iota(i32, (56, 1), 0)
    ce = jnp.where(r < 53, 0.1, jnp.where(r == 53, 1350.0, 1.0)).astype(f32)
    sp = jnp.where(r < 53, 0.06, jnp.where(r == 53, 600.0, 0.1)).astype(f32)
    tail = jnp.where(lax.broadcasted_iota(i32, (8, n), 0) < 2, 1.0, 0.0).astype(f32)
    rr = lax.broadcasted_iota(i32, (56, n), 0)

    up_x, down_x = xpart[0], xpart[nx - 2]
    up_y, down_y = ypart[0], ypart[ny - 2]
    remote = lambda src, dst, a, b, dev: pltpu.make_async_remote_copy(
        src_ref=src, dst_ref=dst, send_sem=a, recv_sem=b, device_id=dev, device_id_type=MESH)
    halos = [remote(ys.at[1], hy.at[0], hsend.at[0], hrecv.at[0], up_y),
             remote(ys.at[0], hy.at[1], hsend.at[1], hrecv.at[1], down_y),
             remote(xs.at[1], hx.at[0], hsend.at[2], hrecv.at[2], up_x),
             remote(xs.at[0], hx.at[1], hsend.at[3], hrecv.at[3], down_x)]
    first = [remote(vmax, s1.at[k], ssem1.at[k], rsem1.at[k], ypart[k]) for k in range(ny - 1)]
    second = [remote(m1, s2.at[k], ssem2.at[k], rsem2.at[k], xpart[k]) for k in range(nx - 1)]

    def exchange(i):
        @pl.when(i == 0)
        def _():
            pl.semaphore_wait(barrier, nx + ny - 2)
            for cp in first + halos:
                cp.start()

        @pl.when(i == 2)
        def _():
            for cp in first:
                cp.wait()
            m1[...] = jnp.maximum(vmax[...], jnp.max(s1[...], axis=0))
            for cp in second:
                cp.start()

    def block(i, c):
        x = jnp.concatenate([packed[NT * i + k] for k in range(NT)], axis=1)
        x = jnp.where(r < 55, (x - ce) / sp, 1.0)
        x = jnp.concatenate([x, tail], axis=0).astype(bf)
        h = act(jnp.dot(w1t[...], x, preferred_element_type=f32), 1.0)
        a = jnp.dot(w2t[...], h, preferred_element_type=f32) + wide(c2[...], n)
        h = act(a, 2.0)
        a = jnp.dot(w3t[...], h, preferred_element_type=f32) + wide(c3[...], n)
        h = act(a, 4.0)
        a = jnp.dot(w4t[...], h, preferred_element_type=f32)
        a = jnp.concatenate([a, jnp.zeros((3, n), f32)], axis=0)
        d = (a + wide(c4[0], n)) * wide(c4[1], n)
        heat = jnp.sum(d * wide(c4[2], n), axis=0, keepdims=True)
        d = jnp.where(rr == 53, heat, d)
        for k in range(NT):
            out[NT * i + k] = d[:, k * 128:(k + 1) * 128]
        exchange(i)
        return c

    lax.fori_loop(0, 32 // NT, block, 0)
    for cp in second:
        cp.wait()
    gm[...] = jnp.maximum(m1[...], jnp.max(s2[...], axis=0))
    for cp in halos:
        cp.wait()


def chem(nx, ny, packed, vmax, xs, ys, w1, b1, w2, b2, w3, b3, w4, b4, inc, hr):
    return pl.pallas_call(
        functools.partial(chem_kernel, nx=nx, ny=ny),
        out_shape=(sd((33, 56, 128), f32), sd((8, 128), f32), sd((2, 448, 256), bf), sd((2, 448, 256), bf)),
        in_specs=[VMEM] * 14,
        out_specs=[VMEM] * 4,
        scratch_shapes=[
            pltpu.VMEM((1600, 64), bf), pltpu.VMEM((800, 128), f32), pltpu.VMEM((400, 128), f32),
            pltpu.VMEM((3, 56, 128), f32),
            pltpu.VMEM((ny - 1, 8, 128), f32), pltpu.VMEM((nx - 1, 8, 128), f32), pltpu.VMEM((8, 128), f32),
            dma((ny - 1,)), dma((ny - 1,)), dma((nx - 1,)), dma((nx - 1,)), dma((4,)), dma((4,)),
        ],
        compiler_params=pltpu.CompilerParams(vmem_limit_bytes=32 << 20, collective_id=0, has_side_effects=True),
        name="chem",
    )(packed, vmax, xs, ys, w1, b1, w2.T, b2, w3.T, b3, w4.T, b4, inc, hr)


def finish_kernel(offs_in, kapv, gm, pos, d, hx, hy, vel, temp, mix, out, tout,
                  coef, ebuf, obuf, hxf, hyf, kcol, offs, sems, osem, *, edges):
    oc = pltpu.make_async_copy(offs_in, offs, osem)
    oc.start()
    flat = ebuf.reshape(2 * HALF, 128)
    lo_x, hi_x, lo_y, hi_y = edges()
    rows = lax.broadcasted_iota(i32, (8, 256), 0)
    lane = lax.broadcasted_iota(i32, (8, 128), 1)
    for k, (fx, fy) in enumerate(((lo_x, lo_y), (hi_x, hi_y))):
        hxf[k] = (hx[k].astype(f32) * fx).reshape(56, 8, 256)
        hyf[k] = (hy[k].astype(f32) * fy).reshape(56, 8, 256)
    kap = kapv[...].reshape(1, 54)
    kcol[...] = col(jnp.concatenate([kap, jnp.zeros((1, 2), f32)], axis=1), 56)
    dt = 0.9 / (jnp.full((8, 256), jnp.max(gm[...])) + 6.0 * jnp.max(kap))
    h = 0.5 * dt
    ux = [hxf[k, 54] + hxf[k, 55] for k in range(2)]
    uy = [hyf[k, 54] + hyf[k, 55] for k in range(2)]
    for x in range(8):
        u0 = vel[0, x]
        u1 = vel[1, x]
        u2 = vel[2, x]
        xp = vel[0, x + 1] if x < 7 else ux[1]
        xm = vel[0, x - 1] if x > 0 else ux[0]
        yp = jnp.where(rows == 7, uy[1][x:x + 1, :], pltpu.roll(u1, 7, 0))
        ym = jnp.where(rows == 0, uy[0][x:x + 1, :], pltpu.roll(u1, 1, 0))
        zp = pltpu.roll(u2, 255, 1)
        zm = pltpu.roll(u2, 1, 1)
        c0 = jnp.ones((8, 256), f32)
        for k, (u, p, q) in enumerate(((u0, xp, xm), (u1, yp, ym), (u2, zp, zm))):
            wp = h * (u + p)
            wm = h * (q + u)
            coef[2 * k, x] = -jnp.minimum(wp, 0.0)
            coef[2 * k + 1, x] = jnp.maximum(wm, 0.0)
            c0 = c0 - (jnp.maximum(wp, 0.0) - jnp.minimum(wm, 0.0))
        coef[6, x] = c0

    oc.wait()

    def group(i, c):
        gs = []
        for k in range(G):
            o = offs[0, i * G + k]
            t = o >> 7
            m = lane >= (o & 127)
            p = jnp.broadcast_to(pos[pl.ds(i * G + k, 1), :], (8, 128))
            q = p & 127
            there = p >= 0
            a = groups(d[t])
            b = groups(d[jnp.minimum(t + 1, 32)])
            gs.append([jnp.where(there, lane_gather(jnp.where(m, x, y), q), 0.0) for x, y in zip(a, b)])
        for k in range(G):
            flat[pl.ds(start_row(i, k), 56, stride=PITCH), :] = jnp.concatenate(gs[k], axis=0)
        return c

    lax.fori_loop(0, 128 // G, group, 0, unroll=4)

    def field(f, load, store):
        kd = jnp.concatenate([kcol[pl.ds(f, 1), :]] * 2, axis=1) * dt
        c6 = 6.0 * kd
        hyl = hyf[0, f]
        hyh = hyf[1, f]
        for x in range(8):
            v = load(x)
            xp = load(x + 1) if x < 7 else hxf[1, f]
            xm = load(x - 1) if x > 0 else hxf[0, f]
            yp = jnp.where(rows == 7, hyh[x:x + 1, :], pltpu.roll(v, 7, 0))
            ym = jnp.where(rows == 0, hyl[x:x + 1, :], pltpu.roll(v, 1, 0))
            zp = pltpu.roll(v, 255, 1)
            zm = pltpu.roll(v, 1, 1)
            acc = (coef[6, x] - c6) * v
            for k, nb in enumerate((xp, xm, yp, ym, zp, zm)):
                acc = acc + (coef[k, x] + kd) * nb
            store(x, acc + jnp.concatenate([ebuf[0, f, x], ebuf[1, f, x]], axis=1))

    def one(f, c):
        def st(x, v):
            obuf[f, x] = v
        field(f, lambda x: mix[f, x], st)
        pltpu.make_async_copy(obuf.at[f], out.at[f], sems.at[f]).start()
        return c

    def stt(x, v):
        obuf[53, x] = v
    field(53, lambda x: temp[x], stt)
    pltpu.make_async_copy(obuf.at[53], tout, sems.at[53]).start()
    lax.fori_loop(0, 53, one, 0, unroll=UF)

    def drain(f, c):
        pltpu.make_async_copy(obuf.at[f], out.at[f], sems.at[f]).wait()
        return c
    lax.fori_loop(0, 53, drain, 0)
    pltpu.make_async_copy(obuf.at[53], tout, sems.at[53]).wait()


def finish(edges, offs, kappa, gm, pos, d, hx, hy, vel, temp, mix):
    return pl.pallas_call(
        functools.partial(finish_kernel, edges=edges),
        out_shape=(sd((53, 8, 8, 256), f32), sd((8, 8, 256), f32)),
        in_specs=[VMEM] * 10,
        out_specs=[HBM, HBM],
        scratch_shapes=[pltpu.VMEM((7, 8, 8, 256), f32), pltpu.VMEM((2, 56, 9, 8, 128), f32),
                        pltpu.VMEM((54, 8, 8, 256), f32), pltpu.VMEM((2, 56, 8, 256), f32),
                        pltpu.VMEM((2, 56, 8, 256), f32), pltpu.VMEM((56, 128), f32), pltpu.SMEM((8, 256), i32),
                        dma((54,)), dma],
        compiler_params=pltpu.CompilerParams(vmem_limit_bytes=24 << 20),
        name="finish",
    )(offs, kappa, gm, pos, d, hx, hy, vel, temp, mix)


def edges(nx, ny):
    gx, yz = lax.axis_index("gx"), lax.axis_index("yz")
    flag = lambda c: jnp.where(c, 1.0, 0.0).astype(f32)
    return flag(gx > 0), flag(gx < nx - 1), flag(yz > 0), flag(yz < ny - 1)


def shards(nx, ny, mix, temp, press, vel, kappa, tally, listing, *weights):
    packed, pos, offs, vmax, xs, ys = prep(tally, listing, mix, temp, press, vel)
    d, gm, hx, hy = chem(nx, ny, packed, vmax, xs, ys, *weights)
    return finish(functools.partial(edges, nx, ny), offs, kappa, gm, pos, d, hx, hy, vel, temp, mix)


def solution(mesh):
    in_specs = (
        P(None, "gx", "yz", None),
        P("gx", "yz", None),
        P("gx", "yz", None),
        P(None, "gx", "yz", None),
        P(),
        P("gx", "yz"),
        P("gx", "yz", None),
    ) + (P(),) * 10
    out_specs = (P(None, "gx", "yz", None), P("gx", "yz", None))
    nx, ny = mesh.shape["gx"], mesh.shape["yz"]
    return jax.shard_map(functools.partial(shards, nx, ny), mesh=mesh, in_specs=in_specs, out_specs=out_specs, check_vma=False)
```

```python
import functools
import math

import jax
import jax.numpy as jnp
from jax import lax
from jax.experimental import pallas as pl
from jax.experimental.pallas import tpu as pltpu
from jax.sharding import PartitionSpec as P

f32 = jnp.float32
bf = jnp.bfloat16
i32 = jnp.int32
C = math.sqrt(2 / math.pi)
MESH = pl.DeviceIdType.MESH
VMEM = pl.BlockSpec(memory_space=pltpu.VMEM)
SMEM = pl.BlockSpec(memory_space=pltpu.SMEM)
HBM = pl.BlockSpec(memory_space=pltpu.HBM)
sd = jax.ShapeDtypeStruct
dma = pltpu.SemaphoreType.DMA
G = 16
NT = 8
UF = 4
PITCH = 72
HALF = 56 * PITCH


def lane_gather(x, idx):
    return jnp.take_along_axis(x, idx, axis=1, mode="promise_in_bounds")


def groups(x):
    return [x[8 * k:8 * k + 8] for k in range(7)]


def start_row(i, k):
    return (k & 1) * HALF + i * (G // 2) + (k >> 1)


def prep_kernel(tally, listing, mix, temp, press, vel,
                packed, pos, offs, vmax, xs, ys,
                buf, velbuf, lst, perm_ref, offs_smem, sems, lsem, osem):
    lc = pltpu.make_async_copy(listing.at[0], lst, lsem)
    lc.start()
    copies = [pltpu.make_async_copy(vel, velbuf, sems.at[6])]
    for j in range(2):
        lanes = pl.ds(128 * j, 128)
        copies.append(pltpu.make_async_copy(mix.at[:, :, :, lanes], buf.at[j, pl.ds(0, 53), pl.ds(0, 8)], sems.at[j]))
        copies.append(pltpu.make_async_copy(temp.at[:, :, lanes], buf.at[j, 53, pl.ds(0, 8)], sems.at[2 + j]))
        copies.append(pltpu.make_async_copy(press.at[:, :, lanes], buf.at[j, 54, pl.ds(0, 8)], sems.at[4 + j]))
    for c in copies:
        c.start()
    buf[0, 55] = jnp.zeros((9, 8, 128), f32)
    buf[1, 55] = jnp.zeros((9, 8, 128), f32)
    n = tally[0, 0]
    lc.wait()
    cells = lst[...]
    slot = lax.broadcasted_iota(i32, (1, 4096), 1)
    hi = jnp.where(slot < n, cells >> 7, -1)
    lo = cells & 127
    rows = lax.broadcasted_iota(i32, (128, 4096), 0)
    a = jnp.where(hi == rows, 1.0, 0.0).astype(bf)
    b = jnp.where(lo == rows, 1.0, 0.0).astype(bf)
    nt = (((1,), (1,)), ((), ()))
    mask = lax.dot_general(a, b, nt, preferred_element_type=f32)
    maskb = mask.astype(bf)
    ri = lax.broadcasted_iota(i32, (128, 128), 0)
    ci = lax.broadcasted_iota(i32, (128, 128), 1)
    before = lax.broadcasted_iota(i32, (128, 256), 0) < lax.broadcasted_iota(i32, (128, 256), 1)
    cntr = lax.dot_general(jnp.ones((8, 128), bf), maskb, nt, preferred_element_type=f32)
    offs[...] = jnp.dot(cntr.astype(bf), jnp.where(before, 1.0, 0.0).astype(bf), preferred_element_type=f32).astype(i32)
    oc = pltpu.make_async_copy(offs, offs_smem, osem)
    oc.start()
    incl = jnp.dot(maskb, jnp.where(ri <= ci, 1.0, 0.0).astype(bf), preferred_element_type=f32)
    cnt = jnp.dot(maskb, jnp.ones((128, 128), bf), preferred_element_type=f32)
    off = jnp.dot(jnp.where(ci < ri, 1.0, 0.0).astype(bf), cnt.astype(bf), preferred_element_type=f32)
    pos[...] = jnp.where(mask > 0.5, (off + incl).astype(i32) - 1, -1)
    want = (((ci - off.astype(i32)) & 127) + 1).astype(f32)
    at = jnp.zeros((128, 128), i32)
    for s in (64, 32, 16, 8, 4, 2, 1):
        v = lane_gather(incl, at + (s - 1))
        at = jnp.where(v < want, at + s, at)
    perm_ref[...] = at
    copies[0].wait()
    s = jnp.abs(velbuf[0]) + jnp.abs(velbuf[1]) + jnp.abs(velbuf[2])
    s = jnp.max(s, axis=0)
    vmax[...] = jnp.maximum(s[:, :128], s[:, 128:])
    for c in copies[1:]:
        c.wait()
    oc.wait()
    flat = buf.reshape(2 * HALF, 128)
    lane = lax.broadcasted_iota(i32, (8, 128), 1)

    def group(i, cur):
        gs = []
        for k in range(G):
            g = flat[pl.ds(start_row(i, k), 56, stride=PITCH), :]
            p = jnp.broadcast_to(perm_ref[pl.ds(i * G + k, 1), :], (8, 128))
            gs.append([lane_gather(x, p) for x in groups(g)])
        for k in range(G):
            o = offs_smem[0, i * G + k]
            t = o >> 7
            m = lane >= (o & 127)
            fresh = (offs_smem[0, i * G + k + 1] >> 7) != t
            cur = [jnp.where(m, g, c) for g, c in zip(gs[k], cur)]
            for q in range(7):
                packed[t, 8 * q:8 * q + 8] = cur[q]
            cur = [jnp.where(fresh, g, c) for g, c in zip(gs[k], cur)]
        return tuple(cur)

    cur = lax.fori_loop(0, 128 // G, group, tuple(jnp.zeros((8, 128), f32) for _ in range(7)), unroll=8)
    for q in range(7):
        packed[n >> 7, 8 * q:8 * q + 8] = cur[q]
    for k, x in enumerate((0, 7)):
        u = velbuf[0, x]
        uh = u.astype(bf).astype(f32)
        xs[k, 432:448] = jnp.concatenate([uh, u - uh], axis=0).astype(bf)
        for j in range(2):
            xs[k, 0:432, 128 * j:128 * j + 128] = buf[j, 0:54, x].reshape(432, 128).astype(bf)
    for k, y in enumerate((0, 7)):
        u = velbuf[1, :, y, :]
        uh = u.astype(bf).astype(f32)
        ys[k, 432:448] = jnp.concatenate([uh, u - uh], axis=0).astype(bf)
        for j in range(2):
            for f in range(0, 54, 2):
                z = [flat[pl.ds(j * HALF + (f + q) * PITCH + y, 8, stride=8), :] for q in range(2)]
                ys[k, 8 * f:8 * f + 16, 128 * j:128 * j + 128] = jnp.concatenate(z, axis=0).astype(bf)


def in_hbm(*arrays):
    return [pltpu.with_memory_space_constraint(a, pltpu.HBM) for a in arrays]


def prep(tally, listing, mix, temp, press, vel):
    return pl.pallas_call(
        prep_kernel,
        out_shape=(sd((33, 56, 128), f32), sd((128, 128), i32), sd((8, 256), i32), sd((8, 128), f32),
                   sd((2, 448, 256), bf), sd((2, 448, 256), bf)),
        in_specs=[SMEM] + [HBM] * 5,
        out_specs=[VMEM] * 6,
        scratch_shapes=[pltpu.VMEM((2, 56, 9, 8, 128), f32), pltpu.VMEM((3, 8, 8, 256), f32), pltpu.VMEM((1, 4096), i32),
                        pltpu.VMEM((128, 128), i32), pltpu.SMEM((8, 256), i32), dma((7,)), dma, dma],
        compiler_params=pltpu.CompilerParams(vmem_limit_bytes=20 << 20),
        name="prep",
    )(tally, *in_hbm(listing, mix, temp, press, vel))


def act(y, s):
    y2 = y * y
    u = y * ((C * 0.044715 / s**3) * y2 + (C / s))
    return (y + y * jnp.tanh(u)).astype(bf)


def col(row, n):
    return jnp.transpose(jnp.broadcast_to(row, (128, n)))


def wide(b, n):
    return jnp.concatenate([b] * (n // 128), axis=1)


def chem_kernel(packed, vmax, xs, ys, w1, b1, w2t, b2, w3t, b3, w4t, b4, inc, hr,
                out, gm, hx, hy,
                w1t, c2, c3, c4, s1, s2, m1, ssem1, rsem1, ssem2, rsem2, hsend, hrecv, *, nx, ny):
    gx, yz = lax.axis_index("gx"), lax.axis_index("yz")
    xpart = [(lax.rem(gx + k, nx), yz) for k in range(1, nx)]
    ypart = [(gx, lax.rem(yz + k, ny)) for k in range(1, ny)]
    barrier = pltpu.get_barrier_semaphore()
    for dev in xpart + ypart:
        pl.semaphore_signal(barrier, inc=1, device_id=dev, device_id_type=MESH)

    b = b1[...].reshape(1, 1600)
    hi = b.astype(bf).astype(f32)
    mid = (b - hi).astype(bf).astype(f32)
    lo = b - hi - mid
    wp = jnp.concatenate([w1[...].astype(f32), hi, mid, lo, jnp.zeros((70, 1600), f32)], axis=0)
    w1t[...] = jnp.transpose(wp)[:, :64].astype(bf)
    c2[...] = col(2.0 * b2[...].reshape(1, 800), 800)
    c3[...] = col(4.0 * b3[...].reshape(1, 400), 400)
    z = jnp.zeros((1, 3), f32)
    c4[0] = col(jnp.concatenate([8.0 * b4[...].reshape(1, 53), z], 1), 56)
    c4[1] = col(jnp.concatenate([inc[...].reshape(1, 53) * 0.125, z], 1), 56)
    c4[2] = col(jnp.concatenate([-hr[...].reshape(1, 53), z], 1), 56)
    n = NT * 128
    r = lax.broadcasted_iota(i32, (56, 1), 0)
    ce = jnp.where(r < 53, 0.1, jnp.where(r == 53, 1350.0, 1.0)).astype(f32)
    sp = jnp.where(r < 53, 0.06, jnp.where(r == 53, 600.0, 0.1)).astype(f32)
    tail = jnp.where(lax.broadcasted_iota(i32, (8, n), 0) < 2, 1.0, 0.0).astype(f32)
    rr = lax.broadcasted_iota(i32, (56, n), 0)

    up_x, down_x = xpart[0], xpart[nx - 2]
    up_y, down_y = ypart[0], ypart[ny - 2]
    remote = lambda src, dst, a, b, dev: pltpu.make_async_remote_copy(
        src_ref=src, dst_ref=dst, send_sem=a, recv_sem=b, device_id=dev, device_id_type=MESH)
    halos = [remote(ys.at[1], hy.at[0], hsend.at[0], hrecv.at[0], up_y),
             remote(ys.at[0], hy.at[1], hsend.at[1], hrecv.at[1], down_y),
             remote(xs.at[1], hx.at[0], hsend.at[2], hrecv.at[2], up_x),
             remote(xs.at[0], hx.at[1], hsend.at[3], hrecv.at[3], down_x)]
    first = [remote(vmax, s1.at[k], ssem1.at[k], rsem1.at[k], xpart[k]) for k in range(nx - 1)]
    second = [remote(m1, s2.at[k], ssem2.at[k], rsem2.at[k], ypart[k]) for k in range(ny - 1)]

    def exchange(i):
        @pl.when(i == 0)
        def _():
            pl.semaphore_wait(barrier, nx + ny - 2)
            for cp in first + halos[:2]:
                cp.start()

        @pl.when(i == 1)
        def _():
            for cp in first:
                cp.wait()
            m1[...] = jnp.maximum(vmax[...], jnp.max(s1[...], axis=0))
            for cp in second + halos[2:]:
                cp.start()

    def block(i, c):
        x = jnp.concatenate([packed[NT * i + k] for k in range(NT)], axis=1)
        x = jnp.where(r < 55, (x - ce) / sp, 1.0)
        x = jnp.concatenate([x, tail], axis=0).astype(bf)
        h = act(jnp.dot(w1t[...], x, preferred_element_type=f32), 1.0)
        a = jnp.dot(w2t[...], h, preferred_element_type=f32) + wide(c2[...], n)
        h = act(a, 2.0)
        a = jnp.dot(w3t[...], h, preferred_element_type=f32) + wide(c3[...], n)
        h = act(a, 4.0)
        a = jnp.dot(w4t[...], h, preferred_element_type=f32)
        a = jnp.concatenate([a, jnp.zeros((3, n), f32)], axis=0)
        d = (a + wide(c4[0], n)) * wide(c4[1], n)
        heat = jnp.sum(d * wide(c4[2], n), axis=0, keepdims=True)
        d = jnp.where(rr == 53, heat, d)
        for k in range(NT):
            out[NT * i + k] = d[:, k * 128:(k + 1) * 128]
        exchange(i)
        return c

    lax.fori_loop(0, 32 // NT, block, 0)
    for cp in second:
        cp.wait()
    gm[...] = jnp.maximum(m1[...], jnp.max(s2[...], axis=0))
    for cp in halos:
        cp.wait()


def chem(nx, ny, packed, vmax, xs, ys, w1, b1, w2, b2, w3, b3, w4, b4, inc, hr):
    return pl.pallas_call(
        functools.partial(chem_kernel, nx=nx, ny=ny),
        out_shape=(sd((33, 56, 128), f32), sd((8, 128), f32), sd((2, 448, 256), bf), sd((2, 448, 256), bf)),
        in_specs=[VMEM] * 14,
        out_specs=[VMEM] * 4,
        scratch_shapes=[
            pltpu.VMEM((1600, 64), bf), pltpu.VMEM((800, 128), f32), pltpu.VMEM((400, 128), f32),
            pltpu.VMEM((3, 56, 128), f32),
            pltpu.VMEM((nx - 1, 8, 128), f32), pltpu.VMEM((ny - 1, 8, 128), f32), pltpu.VMEM((8, 128), f32),
            dma((nx - 1,)), dma((nx - 1,)), dma((ny - 1,)), dma((ny - 1,)), dma((4,)), dma((4,)),
        ],
        compiler_params=pltpu.CompilerParams(vmem_limit_bytes=32 << 20, collective_id=0, has_side_effects=True),
        name="chem",
    )(packed, vmax, xs, ys, w1, b1, w2.T, b2, w3.T, b3, w4.T, b4, inc, hr)


def finish_kernel(offs_in, kapv, gm, pos, d, hx, hy, vel, temp, mix, out, tout,
                  coef, ebuf, obuf, hxf, hyf, kcol, offs, sems, osem, *, edges):
    oc = pltpu.make_async_copy(offs_in, offs, osem)
    oc.start()
    flat = ebuf.reshape(2 * HALF, 128)
    lo_x, hi_x, lo_y, hi_y = edges()
    rows = lax.broadcasted_iota(i32, (8, 256), 0)
    lane = lax.broadcasted_iota(i32, (8, 128), 1)
    for k, (fx, fy) in enumerate(((lo_x, lo_y), (hi_x, hi_y))):
        hxf[k] = (hx[k].astype(f32) * fx).reshape(56, 8, 256)
        hyf[k] = (hy[k].astype(f32) * fy).reshape(56, 8, 256)
    kap = kapv[...].reshape(1, 54)
    kcol[...] = col(jnp.concatenate([kap, jnp.zeros((1, 2), f32)], axis=1), 56)
    dt = 0.9 / (jnp.full((8, 256), jnp.max(gm[...])) + 6.0 * jnp.max(kap))
    h = 0.5 * dt
    ux = [hxf[k, 54] + hxf[k, 55] for k in range(2)]
    uy = [hyf[k, 54] + hyf[k, 55] for k in range(2)]
    for x in range(8):
        u0 = vel[0, x]
        u1 = vel[1, x]
        u2 = vel[2, x]
        xp = vel[0, x + 1] if x < 7 else ux[1]
        xm = vel[0, x - 1] if x > 0 else ux[0]
        yp = jnp.where(rows == 7, uy[1][x:x + 1, :], pltpu.roll(u1, 7, 0))
        ym = jnp.where(rows == 0, uy[0][x:x + 1, :], pltpu.roll(u1, 1, 0))
        zp = pltpu.roll(u2, 255, 1)
        zm = pltpu.roll(u2, 1, 1)
        c0 = jnp.ones((8, 256), f32)
        for k, (u, p, q) in enumerate(((u0, xp, xm), (u1, yp, ym), (u2, zp, zm))):
            wp = h * (u + p)
            wm = h * (q + u)
            coef[2 * k, x] = -jnp.minimum(wp, 0.0)
            coef[2 * k + 1, x] = jnp.maximum(wm, 0.0)
            c0 = c0 - (jnp.maximum(wp, 0.0) - jnp.minimum(wm, 0.0))
        coef[6, x] = c0

    oc.wait()

    def group(i, c):
        gs = []
        for k in range(G):
            o = offs[0, i * G + k]
            t = o >> 7
            m = lane >= (o & 127)
            p = jnp.broadcast_to(pos[pl.ds(i * G + k, 1), :], (8, 128))
            q = p & 127
            there = p >= 0
            a = groups(d[t])
            b = groups(d[jnp.minimum(t + 1, 32)])
            gs.append([jnp.where(there, lane_gather(jnp.where(m, x, y), q), 0.0) for x, y in zip(a, b)])
        for k in range(G):
            flat[pl.ds(start_row(i, k), 56, stride=PITCH), :] = jnp.concatenate(gs[k], axis=0)
        return c

    lax.fori_loop(0, 128 // G, group, 0, unroll=2)

    def field(f, load, store):
        kd = jnp.concatenate([kcol[pl.ds(f, 1), :]] * 2, axis=1) * dt
        c6 = 6.0 * kd
        hyl = hyf[0, f]
        hyh = hyf[1, f]
        for x in range(8):
            v = load(x)
            xp = load(x + 1) if x < 7 else hxf[1, f]
            xm = load(x - 1) if x > 0 else hxf[0, f]
            yp = jnp.where(rows == 7, hyh[x:x + 1, :], pltpu.roll(v, 7, 0))
            ym = jnp.where(rows == 0, hyl[x:x + 1, :], pltpu.roll(v, 1, 0))
            zp = pltpu.roll(v, 255, 1)
            zm = pltpu.roll(v, 1, 1)
            acc = (coef[6, x] - c6) * v
            for k, nb in enumerate((xp, xm, yp, ym, zp, zm)):
                acc = acc + (coef[k, x] + kd) * nb
            store(x, acc + jnp.concatenate([ebuf[0, f, x], ebuf[1, f, x]], axis=1))

    def one(f, c):
        def st(x, v):
            obuf[f, x] = v
        field(f, lambda x: mix[f, x], st)
        pltpu.make_async_copy(obuf.at[f], out.at[f], sems.at[f]).start()
        return c

    def stt(x, v):
        obuf[53, x] = v
    field(53, lambda x: temp[x], stt)
    pltpu.make_async_copy(obuf.at[53], tout, sems.at[53]).start()
    lax.fori_loop(0, 53, one, 0, unroll=UF)

    def drain(f, c):
        pltpu.make_async_copy(obuf.at[f], out.at[f], sems.at[f]).wait()
        return c
    lax.fori_loop(0, 53, drain, 0)
    pltpu.make_async_copy(obuf.at[53], tout, sems.at[53]).wait()


def finish(edges, offs, kappa, gm, pos, d, hx, hy, vel, temp, mix):
    return pl.pallas_call(
        functools.partial(finish_kernel, edges=edges),
        out_shape=(sd((53, 8, 8, 256), f32), sd((8, 8, 256), f32)),
        in_specs=[VMEM] * 10,
        out_specs=[HBM, HBM],
        scratch_shapes=[pltpu.VMEM((7, 8, 8, 256), f32), pltpu.VMEM((2, 56, 9, 8, 128), f32),
                        pltpu.VMEM((54, 8, 8, 256), f32), pltpu.VMEM((2, 56, 8, 256), f32),
                        pltpu.VMEM((2, 56, 8, 256), f32), pltpu.VMEM((56, 128), f32), pltpu.SMEM((8, 256), i32),
                        dma((54,)), dma],
        compiler_params=pltpu.CompilerParams(vmem_limit_bytes=24 << 20),
        name="finish",
    )(offs, kappa, gm, pos, d, hx, hy, vel, temp, mix)


def edges(nx, ny):
    gx, yz = lax.axis_index("gx"), lax.axis_index("yz")
    flag = lambda c: jnp.where(c, 1.0, 0.0).astype(f32)
    return flag(gx > 0), flag(gx < nx - 1), flag(yz > 0), flag(yz < ny - 1)


def shards(nx, ny, mix, temp, press, vel, kappa, tally, listing, *weights):
    packed, pos, offs, vmax, xs, ys = prep(tally, listing, mix, temp, press, vel)
    d, gm, hx, hy = chem(nx, ny, packed, vmax, xs, ys, *weights)
    return finish(functools.partial(edges, nx, ny), offs, kappa, gm, pos, d, hx, hy, vel, temp, mix)


def solution(mesh):
    in_specs = (
        P(None, "gx", "yz", None),
        P("gx", "yz", None),
        P("gx", "yz", None),
        P(None, "gx", "yz", None),
        P(),
        P("gx", "yz"),
        P("gx", "yz", None),
    ) + (P(),) * 10
    out_specs = (P(None, "gx", "yz", None), P("gx", "yz", None))
    nx, ny = mesh.shape["gx"], mesh.shape["yz"]
    return jax.shard_map(functools.partial(shards, nx, ny), mesh=mesh, in_specs=in_specs, out_specs=out_specs, check_vma=False)
```
